256 devices in a mesh: replica: 4 (over z_lo, core), fsdp: 64 (over z_hi, y, x).
Axes of the slice: x: 4, y: 4, z: 8 (z_hi: 4, z_lo: 2; z = z_hi * 2 + z_lo), core: 2. Of those that a mesh axis runs over, the one named last changes fastest.
Arguments:
- outer_gate: float32 [4096, 16384], P('replica', 'fsdp'), may hold values from -6 to 6
- outer_up: float32 [4096, 16384], P('replica', 'fsdp'), may hold values from -6 to 6
- outer_down: float32 [4096, 16384], P('replica', 'fsdp'), may hold values from -6 to 6
- momentum_gate: float32 [4096, 16384], P('replica', 'fsdp'), may hold values from -0.75 to 0.75
- momentum_up: float32 [4096, 16384], P('replica', 'fsdp'), may hold values from -0.75 to 0.75
- momentum_down: float32 [4096, 16384], P('replica', 'fsdp'), may hold values from -0.75 to 0.75
- inputs: bfloat16 [2, 4, 256, 4096], P(None, 'replica', 'fsdp'), may hold values from -6 to 6
- targets: bfloat16 [2, 4, 256, 4096], P(None, 'replica', 'fsdp'), may hold values from -6 to 6
- loss_flags: int32 [2, 4, 256], P(None, 'replica', 'fsdp'), may hold values 0 or 1
Outputs:
- new_gate: float32 [4096, 16384], P('replica', 'fsdp')
- new_up: float32 [4096, 16384], P('replica', 'fsdp')
- new_down: float32 [4096, 16384], P('replica', 'fsdp')
- new_momentum_gate: float32 [4096, 16384], P('replica', 'fsdp')
- new_momentum_up: float32 [4096, 16384], P('replica', 'fsdp')
- new_momentum_down: float32 [4096, 16384], P('replica', 'fsdp')
The draws below stay inside these ranges and needn't reach their ends.
All inputs are finite; a program needn't handle non-finite values. No bound on the sum of `loss_flags` on one device may be relied on, other than what follows from the above.
Results may differ from the reference program's by a relative error of at most 0.012.
Values may be sent and summed in bfloat16 or wider, within the bound.
No kernel may reach another device: no remote copies, remote signals or barrier semaphores. Data moves between devices by JAX's collectives and lax.ppermute only.
A program may use at most 128 MiB of HBM per device.

```python
import math
import jax
import jax.numpy as jnp
from jax import lax

D = 4096
FF = 16384
MB = 256
ITERS = 2
N_REPLICA = 4


def set_ends(values, own_key, least, top_value):
    extent = values.shape
    spot = [jax.random.randint(jax.random.fold_in(own_key, axis), (), 0, extent[axis]) for axis in range(len(extent))]
    values = values.at[tuple(spot)].set(least)
    longest = extent.index(max(extent))
    spot[longest] = (spot[longest] + 1) % extent[longest]
    return values.at[tuple(spot)].set(top_value)


def steps_of(own_key, dims, cuts, least, top_value):
    loudness, own = 1.0, jax.random.fold_in(own_key, 6)
    for axis_at, parts in cuts:
        draws = jnp.exp(jax.random.uniform(jax.random.fold_in(own, axis_at), (parts,), jnp.float32, least / len(cuts), top_value / len(cuts)))
        loudness = loudness * jnp.repeat(draws, dims[axis_at] // parts).reshape([-1 if axis == axis_at else 1 for axis in range(len(dims))])
    return loudness


def centred(rng, shape, width, most, cuts=(), dtype=jnp.bfloat16):
    values = jax.random.normal(rng, shape, jnp.float32) * width
    if len(cuts) > 0:
        values = steps_of(rng, shape, cuts, -0.22, 0.18) * values
    return jnp.clip(values, min=-most, max=most).astype(dtype)


def setup_inputs(seed: int = 0) -> dict:
    key_list = jax.random.split(jax.random.key(seed), 10)
    return {
        "outer_gate": centred(key_list[0], (D, FF), 1.0, 6.0, ((0, 4), (1, 64)), jnp.float32),
        "outer_up": centred(key_list[1], (D, FF), 1.0, 6.0, ((0, 4), (1, 64)), jnp.float32),
        "outer_down": centred(key_list[2], (D, FF), 1.0, 6.0, ((0, 4), (1, 64)), jnp.float32),
        "momentum_gate": centred(key_list[3], (D, FF), 0.05, 0.75, ((0, 4), (1, 64)), jnp.float32),
        "momentum_up": centred(key_list[4], (D, FF), 0.05, 0.75, ((0, 4), (1, 64)), jnp.float32),
        "momentum_down": centred(key_list[5], (D, FF), 0.05, 0.75, ((0, 4), (1, 64)), jnp.float32),
        "inputs": centred(key_list[6], (ITERS, N_REPLICA, MB, D), 1.0, 6.0, ((1, 4), (2, 64))),
        "targets": centred(key_list[7], (ITERS, N_REPLICA, MB, D), 1.0, 6.0, ((1, 4), (2, 64))),
        "loss_flags": set_ends((jax.random.randint(key_list[8], (ITERS, N_REPLICA, MB), 0, 4) < 3).astype(jnp.int32), jax.random.fold_in(key_list[8], 1), 0, 1),
    }


BETA_ONE = 0.9
BETA_TWO = 0.95
INNER_RATE = 0.05
DECAY_RATE = 0.1
OUTER_RATE = 0.7
MOMENTUM_RATE = 0.9

def contract_rows(left, right):
    return lax.dot_general(left, right, (((0,), (0,)), ((), ())), preferred_element_type=jnp.float32)

def contract_cols(left, right):
    return lax.dot_general(left, right, (((1,), (1,)), ((), ())), preferred_element_type=jnp.float32)

def adamw_update(weight, moment, second, grad, count, epsilon):
    moment = BETA_ONE * moment + (1.0 - BETA_ONE) * grad
    second = BETA_TWO * second + (1.0 - BETA_TWO) * grad * grad
    first_hat = moment / (1.0 - BETA_ONE ** count)
    second_hat = second / (1.0 - BETA_TWO ** count)
    weight = weight - INNER_RATE * (first_hat / (jnp.sqrt(second_hat) + epsilon) + DECAY_RATE * weight)
    return (weight, moment, second)

def fragment_grads(weights, batch, target, flags):
    scale_in = D ** (-0.5)
    scale_hidden = FF ** (-0.5)
    w_gate, w_up, w_down = [item.astype(jnp.bfloat16) for item in weights]
    gate_pre = jnp.dot(batch, w_gate, preferred_element_type=jnp.float32) * scale_in
    up_pre = jnp.dot(batch, w_up, preferred_element_type=jnp.float32) * scale_in
    sigma = jax.nn.sigmoid(gate_pre)
    active = gate_pre * sigma
    hidden = (active * up_pre).astype(jnp.bfloat16)
    output = contract_cols(hidden, w_down) * scale_hidden
    out_grad = (flags[:, None] * (output - target.astype(jnp.float32)) / MB).astype(jnp.bfloat16)
    grad_down = contract_rows(out_grad, hidden) * scale_hidden
    hidden_grad = jnp.dot(out_grad, w_down, preferred_element_type=jnp.float32) * scale_hidden
    gate_grad = (hidden_grad * up_pre * sigma * (1.0 + gate_pre * (1.0 - sigma))).astype(jnp.bfloat16)
    up_grad = (hidden_grad * active).astype(jnp.bfloat16)
    grad_gate = contract_rows(batch, gate_grad) * scale_in
    grad_up = contract_rows(batch, up_grad) * scale_in
    return (grad_gate, grad_up, grad_down)

def reference(outer_gate, outer_up, outer_down, momentum_gate, momentum_up, momentum_down, inputs, targets, loss_flags):
    outer = (outer_gate, outer_up, outer_down)
    epsilon = 1.0 / math.sqrt(FF * MB)
    totals = [jnp.zeros_like(item) for item in outer]
    for replica in range(N_REPLICA):
        weights = list(outer)
        moments = [jnp.zeros_like(item) for item in outer]
        seconds = [jnp.zeros_like(item) for item in outer]
        for step in range(ITERS):
            grads = fragment_grads(weights, inputs[step, replica], targets[step, replica], loss_flags[step, replica].astype(jnp.float32))
            for index in range(3):
                weights[index], moments[index], seconds[index] = adamw_update(weights[index], moments[index], seconds[index], grads[index], step + 1, epsilon)
        for index in range(3):
            rounded = lax.optimization_barrier((outer[index] - weights[index]).astype(jnp.bfloat16))
            totals[index] = totals[index] + rounded.astype(jnp.float32)
    momenta = (momentum_gate, momentum_up, momentum_down)
    new_params = []
    new_momenta = []
    for index in range(3):
        average = totals[index] / N_REPLICA
        fresh = MOMENTUM_RATE * momenta[index] + average
        new_momenta.append(fresh)
        new_params.append(outer[index] - OUTER_RATE * (average + MOMENTUM_RATE * fresh))
    return (new_params[0], new_params[1], new_params[2], new_momenta[0], new_momenta[1], new_momenta[2])
```

```python
import math

import jax
import jax.numpy as jnp
from jax import lax
from jax.sharding import Mesh, PartitionSpec as P

ITERS = 2
BETA_ONE = 0.9
BETA_TWO = 0.95
INNER_RATE = 0.05
DECAY_RATE = 0.1
OUTER_RATE = 0.7
MOMENTUM_RATE = 0.9

AXES = ("a", "c", "h", "y", "x")
SIZES = (2, 2, 4, 4, 4)
PLANE = ("y", "x")
BF16 = jnp.bfloat16
F32 = jnp.float32


def contract_rows(left, right):
    return lax.dot_general(
        left, right, (((0,), (0,)), ((), ())), preferred_element_type=F32
    )


def contract_cols(left, right):
    return lax.dot_general(
        left, right, (((1,), (1,)), ((), ())), preferred_element_type=F32
    )


def swap_core(value):
    return lax.ppermute(value, "c", ((0, 1), (1, 0)))


def swap_chip(value):
    return lax.ppermute(value, "a", ((0, 1), (1, 0)))


def relative_blocks(value):
    shape = value.shape
    parts = value.reshape(shape[:-1] + (2, 2, shape[-1] // 4))
    core, chip = lax.axis_index("c"), lax.axis_index("a")
    parts = jnp.where(core == 1, parts[..., ::-1, :], parts)
    parts = jnp.where(chip == 1, parts[..., ::-1, :, :], parts)
    return parts.reshape(shape)


def spread_plane(value):
    copies = lax.psum(1, PLANE)
    return lax.all_to_all(
        jnp.broadcast_to(value[None], (copies,) + value.shape), PLANE, 0, 0
    ).reshape((copies * value.shape[0],) + value.shape[1:])


def sum_plane(value):
    copies = lax.psum(1, PLANE)
    parts = value.reshape((copies, value.shape[0] // copies) + value.shape[1:])
    parts = lax.all_to_all(parts, PLANE, 0, 0)
    return jnp.sum(parts.astype(F32), axis=0)


def sum_height(value):
    sent = value.astype(BF16)
    total = value
    for shift in range(1, SIZES[2]):
        pairs = [(i, (i + shift) % SIZES[2]) for i in range(SIZES[2])]
        total = total + lax.ppermute(sent, "h", pairs).astype(F32)
    return total


def per_device(
    outer_gate,
    outer_up,
    outer_down,
    momentum_gate,
    momentum_up,
    momentum_down,
    inputs,
    targets,
    loss_flags,
):
    tokens = inputs.shape[2]
    features = inputs.shape[3]
    total_rows = tokens * 64
    hidden_units = outer_gate.shape[1] * 64
    scale_in = features ** (-0.5)
    scale_hidden = hidden_units ** (-0.5)
    epsilon = 1.0 / math.sqrt(hidden_units * total_rows)

    own_gu = jnp.stack([outer_gate.astype(BF16), outer_up.astype(BF16)])
    own_d = outer_down.astype(BF16)[None]
    far_gu = swap_chip(own_gu)
    far_d = swap_chip(own_d)
    near_gu = swap_core(own_gu)
    near_d = swap_core(own_d)

    flag_row = jnp.zeros((ITERS, 1, features), BF16)
    flag_row = flag_row.at[:, 0, :tokens].set(loss_flags[:, 0].astype(BF16))
    packed = jnp.concatenate(
        [relative_blocks(inputs[:, 0]), relative_blocks(targets[:, 0]), flag_row], axis=1
    )
    column = lax.all_gather(packed, "h", axis=0)
    column = jnp.swapaxes(column, 0, 1)
    x_rows = column[:, :, :tokens].reshape(ITERS, 4 * tokens, features)
    t_rows = column[:, :, tokens : 2 * tokens].reshape(ITERS, 4 * tokens, features)
    flags = column[:, :, 2 * tokens, :tokens].reshape(ITERS, 4 * tokens).astype(F32)

    batch_one = spread_plane(x_rows[0])
    far_near_gu = swap_core(far_gu)
    far_near_d = swap_core(far_d)
    w_gu = jnp.concatenate([own_gu, near_gu, far_gu, far_near_gu], axis=1)
    w_d = jnp.concatenate([own_d, near_d, far_d, far_near_d], axis=1)
    start = (w_gu[0], w_gu[1], w_d[0])
    batch_two = lax.all_gather(x_rows[1], PLANE, axis=0, tiled=True)

    weights = start
    first = None
    deltas = None
    for step in range(ITERS):
        batch = batch_one if step == 0 else batch_two
        w_gate, w_up, w_down = weights
        gate_pre = jnp.dot(batch, w_gate, preferred_element_type=F32) * scale_in
        up_pre = jnp.dot(batch, w_up, preferred_element_type=F32) * scale_in
        sigma = jax.nn.sigmoid(gate_pre)
        active = gate_pre * sigma
        hidden = (active * up_pre).astype(BF16)
        partial = (contract_cols(hidden, w_down) * scale_hidden).astype(BF16)
        output = sum_height(sum_plane(partial))
        own_grad = (
            flags[step][:, None] * (output - t_rows[step].astype(F32)) / total_rows
        ).astype(BF16)
        out_grad = spread_plane(own_grad)
        grad_down = contract_rows(out_grad, hidden) * scale_hidden
        hidden_grad = jnp.dot(out_grad, w_down, preferred_element_type=F32) * scale_hidden
        gate_grad = (
            hidden_grad * up_pre * sigma * (1.0 + gate_pre * (1.0 - sigma))
        ).astype(BF16)
        up_grad = (hidden_grad * active).astype(BF16)
        grad_gate = contract_rows(batch, gate_grad) * scale_in
        grad_up = contract_rows(batch, up_grad) * scale_in
        grads = (grad_gate, grad_up, grad_down)
        keep = 1.0 - INNER_RATE * DECAY_RATE
        if step == 0:
            first = [item.astype(BF16) for item in grads]
            weights = [
                (
                    keep * w.astype(F32) - INNER_RATE * (g / (jnp.abs(g) + epsilon))
                ).astype(BF16)
                for w, g in zip(start, grads)
            ]
        else:
            m_one = BETA_ONE * (1.0 - BETA_ONE) / (1.0 - BETA_ONE**2)
            m_two = (1.0 - BETA_ONE) / (1.0 - BETA_ONE**2)
            v_one = BETA_TWO * (1.0 - BETA_TWO) / (1.0 - BETA_TWO**2)
            v_two = (1.0 - BETA_TWO) / (1.0 - BETA_TWO**2)
            deltas = []
            for w, p, g in zip(start, first, grads):
                p = p.astype(F32)
                u_one = p / (jnp.abs(p) + epsilon)
                u_two = (m_one * p + m_two * g) / (
                    jnp.sqrt(v_one * p * p + v_two * g * g) + epsilon
                )
                deltas.append(
                    (
                        (1.0 - keep * keep) * w.astype(F32)
                        + (keep * INNER_RATE) * u_one
                        + INNER_RATE * u_two
                    ).astype(BF16)
                )

    outer_own = (outer_gate, outer_up, outer_down)
    momenta = (momentum_gate, momentum_up, momentum_down)
    rows = outer_gate.shape[0]
    new_params = [None] * 3
    new_momenta = [None] * 3
    for index in (2, 0, 1):
        delta = deltas[index].reshape(4, rows, -1)
        near = swap_core(jnp.stack([delta[1], delta[3]]))
        far = swap_chip((delta[2].astype(F32) + near[1].astype(F32)).astype(BF16))
        summed = delta[0].astype(F32) + near[0].astype(F32) + far.astype(F32)
        average = summed / 4.0
        fresh = MOMENTUM_RATE * momenta[index] + average
        new_momenta[index] = fresh
        new_params[index] = outer_own[index] - OUTER_RATE * (
            average + MOMENTUM_RATE * fresh
        )
    return tuple(new_params) + tuple(new_momenta)


def solution(mesh):
    fine = Mesh(mesh.devices.reshape(SIZES), AXES)
    rep, fsdp = ("a", "c"), ("h", "y", "x")
    state = P(rep, fsdp)
    rows = P(None, rep, fsdp, None)
    return jax.shard_map(
        per_device,
        mesh=fine,
        in_specs=(state,) * 6 + (rows, rows, P(None, rep, fsdp)),
        out_specs=(state,) * 6,
        check_vma=False,
    )
```

```python
import math

import jax
import jax.numpy as jnp
from jax import lax
from jax.sharding import Mesh, PartitionSpec as P

ITERS = 2
BETA_ONE = 0.9
BETA_TWO = 0.95
INNER_RATE = 0.05
DECAY_RATE = 0.1
OUTER_RATE = 0.7
MOMENTUM_RATE = 0.9

AXES = ("a", "c", "h", "y", "u", "v")
SIZES = (2, 2, 4, 4, 2, 2)
HEIGHT = 4
PLANE = ("y", "u")
BF16 = jnp.bfloat16
F32 = jnp.float32
SWAP = ((0, 1), (1, 0))
HEIGHT_PAIRS = (((0, 1), (1, 0), (2, 3), (3, 2)), ((0, 3), (3, 0), (1, 2), (2, 1)))


def contract_rows(left, right):
    return lax.dot_general(
        left, right, (((0,), (0,)), ((), ())), preferred_element_type=F32
    )


def contract_cols(left, right):
    return lax.dot_general(
        left, right, (((1,), (1,)), ((), ())), preferred_element_type=F32
    )


def after(value, *others):
    return lax.optimization_barrier((value,) + others)[0]


def own_first(value):
    count, width = value.shape
    parts = value.reshape(count, 2, 2, width // 4)
    parts = jnp.where(lax.axis_index("c") == 1, parts[:, :, ::-1], parts)
    return parts.reshape(count, 2, width // 2)


def regroup(value):
    column = lax.axis_index("v")
    pieces = []
    for flip, pairs in (
        (0, ((0, 0), (1, 2), (2, 1), (3, 3))),
        (1, ((0, 2), (1, 0), (2, 3), (3, 1))),
    ):
        part = lax.dynamic_index_in_dim(value, column ^ flip, 1, keepdims=False)
        pieces.append(lax.ppermute(part, ("a", "v"), pairs))
    low = lax.axis_index("a") == 0
    return jnp.stack(
        [
            jnp.where(low, pieces[0], pieces[1]),
            jnp.where(low, pieces[1], pieces[0]),
        ]
    )


def gather_height(value):
    place = lax.axis_index("h")
    value = value[None]
    for pairs, low in zip(HEIGHT_PAIRS, (place % 2 == 0, place < 2)):
        other = lax.ppermute(value, "h", pairs)
        value = jnp.concatenate(
            [jnp.where(low, value, other), jnp.where(low, other, value)], axis=0
        )
    return value


def spread_plane(value):
    copies = lax.psum(1, PLANE)
    return lax.all_to_all(
        jnp.broadcast_to(value[None], (copies,) + value.shape), PLANE, 0, 0
    ).reshape((copies * value.shape[0],) + value.shape[1:])


def sum_plane(value):
    copies = lax.psum(1, PLANE)
    parts = value.reshape((copies, value.shape[0] // copies) + value.shape[1:])
    parts = lax.all_to_all(parts, PLANE, 0, 0)
    return jnp.sum(parts.astype(F32), axis=0)


def sum_height(value):
    for pairs in HEIGHT_PAIRS:
        value = value + lax.ppermute(value.astype(BF16), "h", pairs).astype(F32)
    return value


def other_half(value):
    return lax.ppermute(value.astype(BF16), "a", SWAP)


def per_device(
    outer_gate,
    outer_up,
    outer_down,
    momentum_gate,
    momentum_up,
    momentum_down,
    inputs,
    targets,
    loss_flags,
):
    tokens = inputs.shape[2]
    features = inputs.shape[3]
    rows, width = outer_gate.shape
    half = features // 2
    group = 2 * HEIGHT * tokens
    total_rows = tokens * 64
    hidden_units = width * 64
    scale_in = features ** (-0.5)
    scale_hidden = hidden_units ** (-0.5)
    epsilon = 1.0 / math.sqrt(hidden_units * total_rows)

    flag_rows = jnp.zeros((ITERS, 2, half), BF16)
    flag_rows = flag_rows.at[:, :, :tokens].set(
        loss_flags[:, 0].astype(BF16)[:, None, :]
    )
    packed = jnp.concatenate(
        [
            own_first(
                jnp.concatenate(
                    [inputs[0, 0], inputs[1, 0], targets[0, 0], targets[1, 0]], axis=0
                )
            ),
            flag_rows,
        ],
        axis=0,
    )
    packed = regroup(packed)

    own = jnp.stack([outer_gate, outer_up, outer_down]).astype(BF16)
    own, packed = lax.optimization_barrier((own, packed))
    side = lax.ppermute(own, "v", SWAP)
    near = lax.ppermute(own, "c", SWAP)

    column = gather_height(packed)
    x_rows = [
        column[:, :, s * tokens : (1 + s) * tokens].reshape(group, half)
        for s in range(ITERS)
    ]
    t_rows = [
        column[:, :, (2 + s) * tokens : (3 + s) * tokens].reshape(group, half)
        for s in range(ITERS)
    ]
    flags = [
        column[:, :, 4 * tokens + s, :tokens].reshape(group, 1).astype(F32)
        for s in range(ITERS)
    ]
    x_first, side = lax.optimization_barrier((x_rows[0], side))
    batch_one = spread_plane(x_first)
    near_side = lax.ppermute(side, "c", SWAP)
    start = [
        [
            jnp.concatenate([own[index], near[index]], axis=0),
            jnp.concatenate([side[index], near_side[index]], axis=0),
        ]
        for index in range(3)
    ]

    keep = 1.0 - INNER_RATE * DECAY_RATE
    m_one = BETA_ONE * (1.0 - BETA_ONE) / (1.0 - BETA_ONE**2)
    m_two = (1.0 - BETA_ONE) / (1.0 - BETA_ONE**2)
    v_one = BETA_TWO * (1.0 - BETA_TWO) / (1.0 - BETA_TWO**2)
    v_two = (1.0 - BETA_TWO) / (1.0 - BETA_TWO**2)

    def first_update(w, g):
        return (
            keep * w.astype(F32) - INNER_RATE * (g / (jnp.abs(g) + epsilon))
        ).astype(BF16)

    def both_updates(w, p, g):
        p = p.astype(F32)
        u_one = p / (jnp.abs(p) + epsilon)
        u_two = (m_one * p + m_two * g) / (
            jnp.sqrt(v_one * p * p + v_two * g * g) + epsilon
        )
        return (
            (1.0 - keep * keep) * w.astype(F32)
            + (keep * INNER_RATE) * u_one
            + INNER_RATE * u_two
        ).astype(BF16)

    def partial_pre(batch, w_gate, w_up):
        return jnp.stack(
            [
                jnp.dot(batch, w_gate, preferred_element_type=F32),
                jnp.dot(batch, w_up, preferred_element_type=F32),
            ]
        )

    def gated(pre):
        return (pre[0] * jax.nn.sigmoid(pre[0]) * pre[1]).astype(BF16)

    def output_sum(hidden, w_down):
        partial = contract_cols(hidden[0], w_down[0]) + contract_cols(
            hidden[1], w_down[1]
        )
        return sum_plane((partial * scale_hidden).astype(BF16))

    def hidden_partial(out_grad, w_down):
        return jnp.stack(
            [jnp.dot(out_grad, w, preferred_element_type=F32) for w in w_down]
        )

    def hidden_grads(hidden_grad, pre):
        hidden_grad = hidden_grad * scale_hidden
        pairs = []
        for side in range(2):
            gate_pre, up_pre = pre[side][0], pre[side][1]
            sigma = jax.nn.sigmoid(gate_pre)
            gate_grad = (
                hidden_grad[side] * up_pre * sigma * (1.0 + gate_pre * (1.0 - sigma))
            ).astype(BF16)
            up_grad = (hidden_grad[side] * (gate_pre * sigma)).astype(BF16)
            pairs.append((gate_grad, up_grad))
        return pairs

    sides = range(2)
    partial = [partial_pre(batch_one, start[0][k], start[1][k]) for k in sides]
    def own_grad(step, total):
        return (
            flags[step] * (total - t_rows[step].astype(F32)) / total_rows
        ).astype(BF16)

    others = [other_half(item) for item in partial]
    batch_two = spread_plane(after(x_rows[1], *partial))
    others = after(others, batch_two)
    pre = [(partial[k] + others[k].astype(F32)) * scale_in for k in sides]
    hidden = [gated(item) for item in pre]
    out_grad = spread_plane(own_grad(0, sum_height(output_sum(hidden, start[2]))))
    partial = hidden_partial(out_grad, start[2])
    pairs = hidden_grads(partial + other_half(partial).astype(F32), pre)
    grads = [
        [contract_rows(batch_one, pairs[k][0]) * scale_in for k in sides],
        [contract_rows(batch_one, pairs[k][1]) * scale_in for k in sides],
        [
            contract_rows(after(out_grad, partial), hidden[k]) * scale_hidden
            for k in sides
        ],
    ]
    weights = [[first_update(start[i][k], grads[i][k]) for k in sides] for i in range(3)]
    first = [[grads[i][k].astype(BF16) for k in sides] for i in range(3)]

    partial = [partial_pre(batch_two, weights[0][k], weights[1][k]) for k in sides]
    pre = [(item + other_half(item).astype(F32)) * scale_in for item in partial]
    hidden = [gated(item) for item in pre]
    out_grad = spread_plane(own_grad(1, sum_height(output_sum(hidden, weights[2]))))
    partial = hidden_partial(out_grad, weights[2])
    other = other_half(partial)
    out_grad = after(out_grad, partial)

    def update(index, side, left, right, scale):
        return both_updates(
            start[index][side], first[index][side], contract_rows(left, right) * scale
        )

    def own_rows(delta):
        near = lax.ppermute(delta[rows:], "c", SWAP)
        return delta[:rows].astype(F32) + near.astype(F32)

    partner = [None] * 3
    delta = update(2, 1, out_grad, hidden[1], scale_hidden)
    sent = own_rows(delta).astype(BF16)
    partner[2] = lax.ppermute(sent, "v", SWAP)
    pairs = hidden_grads(partial + after(other, partner[2]).astype(F32), pre)
    delta = update(0, 1, batch_two, pairs[1][0], scale_in)
    sent_gate = own_rows(delta).astype(BF16)
    partner[0] = lax.ppermute(sent_gate, "v", SWAP)
    delta = update(1, 1, after(batch_two, delta), pairs[1][1], scale_in)
    sent = own_rows(delta).astype(BF16)
    partner[1] = lax.ppermute(sent, "v", SWAP)
    batch_two, out_grad = after((batch_two, out_grad), sent_gate, sent)
    left = {0: batch_two, 1: batch_two, 2: out_grad}
    right = {0: pairs[0][0], 1: pairs[0][1], 2: hidden[0]}
    scales = {0: scale_in, 1: scale_in, 2: scale_hidden}
    outer_own = (outer_gate, outer_up, outer_down)
    momenta = (momentum_gate, momentum_up, momentum_down)
    new_params = [None] * 3
    new_momenta = [None] * 3
    for index in (2, 0, 1):
        delta = update(index, 0, left[index], right[index], scales[index])
        total = own_rows(delta) + partner[index].astype(F32)
        average = total / 4.0
        fresh = MOMENTUM_RATE * momenta[index] + average
        new_momenta[index] = fresh
        new_params[index] = outer_own[index] - OUTER_RATE * (
            average + MOMENTUM_RATE * fresh
        )
    return tuple(new_params) + tuple(new_momenta)


def solution(mesh):
    fine = Mesh(mesh.devices.reshape(SIZES), AXES)
    rep, fsdp = AXES[:2], AXES[2:]
    state = P(rep, fsdp)
    rows = P(None, rep, fsdp, None)
    return jax.shard_map(
        per_device,
        mesh=fine,
        in_specs=(state,) * 6 + (rows, rows, P(None, rep, fsdp)),
        out_specs=(state,) * 6,
        check_vma=False,
    )
```

```python
import functools
import math

import jax
import jax.numpy as jnp
from jax import lax
from jax.experimental import pallas as pl
from jax.experimental.pallas import tpu as pltpu
from jax.sharding import Mesh, PartitionSpec as P

ITERS = 2
BETA_ONE = 0.9
BETA_TWO = 0.95
INNER_RATE = 0.05
DECAY_RATE = 0.1
OUTER_RATE = 0.7
MOMENTUM_RATE = 0.9

AXES = ("a", "c", "h", "y", "u", "v")
SIZES = (2, 2, 4, 4, 2, 2)
HEIGHT = 4
PLANE = ("y", "u")
BF16 = jnp.bfloat16
F32 = jnp.float32
SWAP = ((0, 1), (1, 0))
HEIGHT_PAIRS = (((0, 1), (1, 0), (2, 3), (3, 2)), ((0, 3), (3, 0), (1, 2), (2, 1)))


def contract_rows(left, right):
    return lax.dot_general(
        left, right, (((0,), (0,)), ((), ())), preferred_element_type=F32
    )


def contract_cols(left, right):
    return lax.dot_general(
        left, right, (((1,), (1,)), ((), ())), preferred_element_type=F32
    )


def after(value, *others):
    return lax.optimization_barrier((value,) + others)[0]


def regroup(value):
    column, core = lax.axis_index("v"), lax.axis_index("c")
    width = value.shape[1] // 4
    pieces = []
    for flip, pairs in (
        (0, ((0, 0), (1, 2), (2, 1), (3, 3))),
        (1, ((0, 2), (1, 0), (2, 3), (3, 1))),
    ):
        first = 2 * (column ^ flip) + core
        part = jnp.concatenate(
            [
                lax.dynamic_slice_in_dim(value, first * width, width, 1),
                lax.dynamic_slice_in_dim(value, (first ^ 1) * width, width, 1),
            ],
            axis=1,
        )
        pieces.append((part, pairs))
    parts = lax.optimization_barrier([part for part, _ in pieces])
    pieces = [
        lax.ppermute(part, ("a", "v"), pairs)
        for part, (_, pairs) in zip(parts, pieces)
    ]
    low = lax.axis_index("a") == 0
    return jnp.stack(
        [
            jnp.where(low, pieces[0], pieces[1]),
            jnp.where(low, pieces[1], pieces[0]),
        ]
    )


def gather_height(value):
    place = lax.axis_index("h")
    value = value[None]
    for pairs, low in zip(HEIGHT_PAIRS, (place % 2 == 0, place < 2)):
        other = lax.ppermute(value, "h", pairs)
        value = jnp.concatenate(
            [jnp.where(low, value, other), jnp.where(low, other, value)], axis=0
        )
    return value


def spread_plane(value):
    copies = lax.psum(1, PLANE)
    return lax.all_to_all(
        jnp.broadcast_to(value[None], (copies,) + value.shape), PLANE, 0, 0
    ).reshape((copies * value.shape[0],) + value.shape[1:])


def sum_plane(value):
    copies = lax.psum(1, PLANE)
    parts = value.reshape((copies, value.shape[0] // copies) + value.shape[1:])
    parts = lax.all_to_all(parts, PLANE, 0, 0)
    return jnp.sum(parts.astype(F32), axis=0)


def sum_height(value):
    for pairs in HEIGHT_PAIRS:
        value = value + lax.ppermute(value.astype(BF16), "h", pairs).astype(F32)
    return value


def other_half(value):
    return lax.ppermute(value.astype(BF16), "a", SWAP)


def per_device(
    outer_gate,
    outer_up,
    outer_down,
    momentum_gate,
    momentum_up,
    momentum_down,
    inputs,
    targets,
    loss_flags,
):
    tokens = inputs.shape[2]
    features = inputs.shape[3]
    rows, width = outer_gate.shape
    half = features // 2
    group = 2 * HEIGHT * tokens
    total_rows = tokens * 64
    hidden_units = width * 64
    scale_in = features ** (-0.5)
    scale_hidden = hidden_units ** (-0.5)
    epsilon = 1.0 / math.sqrt(hidden_units * total_rows)

    flag_rows = jnp.zeros((ITERS, 4, half // 2), BF16)
    flag_rows = flag_rows.at[:, :, :tokens].set(
        loss_flags[:, 0].astype(BF16)[:, None, :]
    )
    packed = jnp.concatenate(
        [
            inputs[0, 0],
            inputs[1, 0],
            targets[0, 0],
            targets[1, 0],
            flag_rows.reshape(ITERS, features),
        ],
        axis=0,
    )

    packed = regroup(packed)
    own = jnp.stack([outer_gate, outer_up, outer_down]).astype(BF16)
    own, packed = lax.optimization_barrier((own, packed))
    side = lax.ppermute(own, "v", SWAP)
    near = lax.ppermute(own, "c", SWAP)

    column = gather_height(packed)
    x_rows = [
        column[:, :, s * tokens : (1 + s) * tokens].reshape(group, half)
        for s in range(ITERS)
    ]
    t_rows = [
        column[:, :, (2 + s) * tokens : (3 + s) * tokens].reshape(group, half)
        for s in range(ITERS)
    ]
    flags = [
        column[:, :, 4 * tokens + s, :tokens].reshape(group, 1).astype(F32)
        for s in range(ITERS)
    ]
    x_first, side, near = lax.optimization_barrier((x_rows[0], side, near))
    batch_one = spread_plane(x_first)
    near_side = lax.ppermute(side, "c", SWAP)
    start = [
        [
            jnp.concatenate([own[index], near[index]], axis=0),
            jnp.concatenate([side[index], near_side[index]], axis=0),
        ]
        for index in range(3)
    ]

    keep = 1.0 - INNER_RATE * DECAY_RATE
    m_one = BETA_ONE * (1.0 - BETA_ONE) / (1.0 - BETA_ONE**2)
    m_two = (1.0 - BETA_ONE) / (1.0 - BETA_ONE**2)
    v_one = BETA_TWO * (1.0 - BETA_TWO) / (1.0 - BETA_TWO**2)
    v_two = (1.0 - BETA_TWO) / (1.0 - BETA_TWO**2)

    def first_update(w, g):
        return (
            keep * w.astype(F32) - INNER_RATE * (g / (jnp.abs(g) + epsilon))
        ).astype(BF16)

    def pseudo_gradient(weight, before, raw, scale):
        p = before.astype(F32)
        v = v_one * (p * p) + (v_two * scale * scale) * (raw * raw)
        first_low = jnp.abs(p) + epsilon
        second_low = v * lax.rsqrt(v + 1e-37) + epsilon
        moment = (INNER_RATE * m_one) * p + (INNER_RATE * m_two * scale) * raw
        top = (keep * INNER_RATE) * p * second_low + moment * first_low
        return (
            (1.0 - keep * keep) * weight.astype(F32) + top / (first_low * second_low)
        ).astype(BF16)

    def update_kernel(
        left, right, own_weight, near_weight, before, own_delta, near_delta, *, scale
    ):
        def write(weight, delta):
            for chunk in range(4):
                lines = pl.ds(chunk * (rows // 4), rows // 4)
                raw = contract_rows(left[:, lines], right[...])
                delta[lines] = pseudo_gradient(weight[lines], before[lines], raw, scale)

        @pl.when(pl.program_id(0) == 0)
        def _():
            write(near_weight, near_delta)

        @pl.when(pl.program_id(0) == 1)
        def _():
            write(own_weight, own_delta)

    def update(index, which, left, right, scale):
        deep = left.shape[0]
        whole = pl.BlockSpec((rows, width), lambda i: (0, 0))
        stacked = pl.BlockSpec((None, rows, width), lambda i: (index, 0, 0))
        return pl.pallas_call(
            functools.partial(update_kernel, scale=scale),
            grid=(2,),
            in_specs=[
                pl.BlockSpec((deep, rows), lambda i: (0, 1 - i)),
                pl.BlockSpec((deep, width), lambda i: (0, 0)),
                stacked,
                stacked,
                pl.BlockSpec((rows, width), lambda i: (1 - i, 0)),
            ],
            out_specs=[whole, whole],
            out_shape=[jax.ShapeDtypeStruct((rows, width), BF16)] * 2,
            cost_estimate=pl.CostEstimate(flops=1, bytes_accessed=1, transcendentals=0),
            compiler_params=pltpu.CompilerParams(vmem_limit_bytes=12 * 2**20),
        )(left, right, *((side, near_side) if which else (own, near)), first[index][which])

    def partial_pre(batch, w_gate, w_up):
        return jnp.stack(
            [
                jnp.dot(batch, w_gate, preferred_element_type=F32),
                jnp.dot(batch, w_up, preferred_element_type=F32),
            ]
        )

    def gated(pre):
        return (pre[0] * jax.nn.sigmoid(pre[0]) * pre[1]).astype(BF16)

    def output_sum(hidden, w_down):
        partial = contract_cols(hidden[0], w_down[0]) + contract_cols(
            hidden[1], w_down[1]
        )
        return sum_plane((partial * scale_hidden).astype(BF16))

    def hidden_partial(out_grad, w_down):
        return jnp.stack(
            [jnp.dot(out_grad, w, preferred_element_type=F32) for w in w_down]
        )

    def hidden_grads(partial, other, pre):
        hidden_grad = (partial + other.astype(F32)) * scale_hidden
        gate_pre, up_pre = pre[0], pre[1]
        sigma = jax.nn.sigmoid(gate_pre)
        gate_grad = (
            hidden_grad * up_pre * sigma * (1.0 + gate_pre * (1.0 - sigma))
        ).astype(BF16)
        up_grad = (hidden_grad * (gate_pre * sigma)).astype(BF16)
        return gate_grad, up_grad

    sides = range(2)
    partial = [partial_pre(batch_one, start[0][k], start[1][k]) for k in sides]
    def own_grad(step, total):
        return (
            flags[step] * (total - t_rows[step].astype(F32)) / total_rows
        ).astype(BF16)

    others = [other_half(item) for item in partial]
    batch_two = spread_plane(after(x_rows[1], *partial))
    others = after(others, batch_two)
    pre = [(partial[k] + others[k].astype(F32)) * scale_in for k in sides]
    hidden = [gated(item) for item in pre]
    out_grad = spread_plane(own_grad(0, sum_height(output_sum(hidden, start[2]))))
    partial = hidden_partial(out_grad, start[2])
    other = other_half(partial)
    pairs = [hidden_grads(partial[k], other[k], pre[k]) for k in sides]
    grads = [
        [contract_rows(batch_one, pairs[k][0]) * scale_in for k in sides],
        [contract_rows(batch_one, pairs[k][1]) * scale_in for k in sides],
        [
            contract_rows(after(out_grad, partial), hidden[k]) * scale_hidden
            for k in sides
        ],
    ]
    weights = [[first_update(start[i][k], grads[i][k]) for k in sides] for i in range(3)]
    first = [[grads[i][k].astype(BF16) for k in sides] for i in range(3)]

    partial = [partial_pre(batch_two, weights[0][k], weights[1][k]) for k in sides]
    pre = [(item + other_half(item).astype(F32)) * scale_in for item in partial]
    hidden = [gated(item) for item in pre]
    out_grad = spread_plane(own_grad(1, sum_height(output_sum(hidden, weights[2]))))
    partial = [
        jnp.dot(out_grad, w, preferred_element_type=F32) for w in weights[2]
    ]
    other = [None, other_half(partial[1])]
    other[0] = other_half(after(partial[0], partial[1]))
    out_grad = after(out_grad, *partial)

    outer_own = (outer_gate, outer_up, outer_down)
    momenta = (momentum_gate, momentum_up, momentum_down)

    def both_cores(delta, near, *others):
        near = after(lax.ppermute(near, "c", SWAP), *others)
        return (delta.astype(F32) + near.astype(F32)).astype(BF16)

    delta = pseudo_gradient(
        start[2][1], first[2][1], contract_rows(out_grad, hidden[1]), scale_hidden
    )
    sent = both_cores(delta[:rows], delta[rows:])
    far_down = lax.ppermute(sent, "v", SWAP)
    pairs = [None, hidden_grads(partial[1], after(other[1], sent), pre[1])]
    sent_gate = both_cores(*update(0, 1, batch_two, pairs[1][0], scale_in))
    far_gate = lax.ppermute(sent_gate, "v", SWAP)
    sent_up = both_cores(*update(1, 1, batch_two, pairs[1][1], scale_in), far_down)
    far_up = lax.ppermute(sent_up, "v", SWAP)
    far = [far_gate, far_up, far_down]
    pairs[0] = hidden_grads(partial[0], after(other[0], sent_gate), pre[0])
    batch_two, out_grad = after((batch_two, out_grad), sent_gate, sent_up)
    new_params = [None] * 3
    new_momenta = [None] * 3
    for index, left, right, scale in (
        (2, out_grad, hidden[0], scale_hidden),
        (0, batch_two, pairs[0][0], scale_in),
        (1, batch_two, pairs[0][1], scale_in),
    ):
        own_delta, near_delta = update(index, 0, left, right, scale)
        near_delta = lax.ppermute(near_delta, "c", SWAP)
        total = (
            own_delta.astype(F32) + near_delta.astype(F32) + far[index].astype(F32)
        )
        average = total / 4.0
        fresh = MOMENTUM_RATE * momenta[index] + average
        new_momenta[index] = fresh
        new_params[index] = outer_own[index] - OUTER_RATE * (
            average + MOMENTUM_RATE * fresh
        )
    return tuple(new_params) + tuple(new_momenta)


def solution(mesh):
    fine = Mesh(mesh.devices.reshape(SIZES), AXES)
    rep, fsdp = AXES[:2], AXES[2:]
    state = P(rep, fsdp)
    rows = P(None, rep, fsdp, None)
    return jax.shard_map(
        per_device,
        mesh=fine,
        in_specs=(state,) * 6 + (rows, rows, P(None, rep, fsdp)),
        out_specs=(state,) * 6,
        check_vma=False,
    )
```

```python
import functools
import math

import jax
import jax.numpy as jnp
from jax import lax
from jax.experimental import pallas as pl
from jax.experimental.pallas import tpu as pltpu
from jax.sharding import Mesh, PartitionSpec as P

ITERS = 2
BETA_ONE = 0.9
BETA_TWO = 0.95
INNER_RATE = 0.05
DECAY_RATE = 0.1
OUTER_RATE = 0.7
MOMENTUM_RATE = 0.9

AXES = ("a", "c", "h", "y", "u", "v")
SIZES = (2, 2, 4, 4, 2, 2)
HEIGHT = 4
PLANE = ("y", "u")
BF16 = jnp.bfloat16
F32 = jnp.float32
SWAP = ((0, 1), (1, 0))
HEIGHT_PAIRS = (((0, 1), (1, 0), (2, 3), (3, 2)), ((0, 3), (3, 0), (1, 2), (2, 1)))


def contract_rows(left, right):
    return lax.dot_general(
        left, right, (((0,), (0,)), ((), ())), preferred_element_type=F32
    )


def contract_cols(left, right):
    return lax.dot_general(
        left, right, (((1,), (1,)), ((), ())), preferred_element_type=F32
    )


def after(value, *others):
    return lax.optimization_barrier((value,) + others)[0]


def regroup(value):
    column, core = lax.axis_index("v"), lax.axis_index("c")
    width = value.shape[1] // 4
    pieces = []
    for flip, pairs in (
        (0, ((0, 0), (1, 2), (2, 1), (3, 3))),
        (1, ((0, 2), (1, 0), (2, 3), (3, 1))),
    ):
        first = 2 * (column ^ flip) + core
        part = jnp.concatenate(
            [
                lax.dynamic_slice_in_dim(value, first * width, width, 1),
                lax.dynamic_slice_in_dim(value, (first ^ 1) * width, width, 1),
            ],
            axis=1,
        )
        pieces.append((part, pairs))
    parts = lax.optimization_barrier([part for part, _ in pieces])
    pieces = [
        lax.ppermute(part, ("a", "v"), pairs)
        for part, (_, pairs) in zip(parts, pieces)
    ]
    low = lax.axis_index("a") == 0
    return jnp.stack(
        [
            jnp.where(low, pieces[0], pieces[1]),
            jnp.where(low, pieces[1], pieces[0]),
        ]
    )


def gather_height(value):
    place = lax.axis_index("h")
    value = value[None]
    for pairs, low in zip(HEIGHT_PAIRS, (place % 2 == 0, place < 2)):
        other = lax.ppermute(value, "h", pairs)
        value = jnp.concatenate(
            [jnp.where(low, value, other), jnp.where(low, other, value)], axis=0
        )
    return value


def spread_plane(value):
    copies = lax.psum(1, PLANE)
    return lax.all_to_all(
        jnp.broadcast_to(value[None], (copies,) + value.shape), PLANE, 0, 0
    ).reshape((copies * value.shape[0],) + value.shape[1:])


def sum_plane(value):
    copies = lax.psum(1, PLANE)
    parts = value.reshape((copies, value.shape[0] // copies) + value.shape[1:])
    parts = lax.all_to_all(parts, PLANE, 0, 0)
    return jnp.sum(parts.astype(F32), axis=0)


def sum_height(value):
    for pairs in HEIGHT_PAIRS:
        value = value + lax.ppermute(value.astype(BF16), "h", pairs).astype(F32)
    return value


def other_half(value):
    return lax.ppermute(value.astype(BF16), "a", SWAP)


def per_device(
    outer_gate,
    outer_up,
    outer_down,
    momentum_gate,
    momentum_up,
    momentum_down,
    inputs,
    targets,
    loss_flags,
):
    tokens = inputs.shape[2]
    features = inputs.shape[3]
    rows, width = outer_gate.shape
    half = features // 2
    group = 2 * HEIGHT * tokens
    total_rows = tokens * 64
    hidden_units = width * 64
    scale_in = features ** (-0.5)
    scale_hidden = hidden_units ** (-0.5)
    epsilon = 1.0 / math.sqrt(hidden_units * total_rows)

    flag_rows = jnp.zeros((ITERS, 4, half // 2), BF16)
    flag_rows = flag_rows.at[:, :, :tokens].set(
        loss_flags[:, 0].astype(BF16)[:, None, :]
    )
    packed = jnp.concatenate(
        [
            inputs[0, 0],
            inputs[1, 0],
            targets[0, 0],
            targets[1, 0],
            flag_rows.reshape(ITERS, features),
        ],
        axis=0,
    )

    packed = regroup(packed)
    own = jnp.stack([outer_gate, outer_up, outer_down]).astype(BF16)
    own, packed = lax.optimization_barrier((own, packed))
    side = lax.ppermute(own[:2], "v", SWAP)
    side_down = lax.ppermute(own[2], "v", SWAP)
    near = lax.ppermute(own, "c", SWAP)

    column = gather_height(packed)
    x_rows = [
        column[:, :, s * tokens : (1 + s) * tokens].reshape(group, half)
        for s in range(ITERS)
    ]
    t_rows = [
        column[:, :, (2 + s) * tokens : (3 + s) * tokens].reshape(group, half)
        for s in range(ITERS)
    ]
    flags = [
        column[:, :, 4 * tokens + s, :tokens].reshape(group, 1).astype(F32)
        for s in range(ITERS)
    ]
    x_first, side, near = lax.optimization_barrier((x_rows[0], side, near))
    batch_one = spread_plane(x_first)
    near_side = lax.ppermute(side, "c", SWAP)
    x_second, side_down = lax.optimization_barrier((x_rows[1], side_down))
    sides_of = (
        (side[0], near_side[0]),
        (side[1], near_side[1]),
        (side_down, lax.ppermute(side_down, "c", SWAP)),
    )
    start = [
        [
            jnp.concatenate([own[index], near[index]], axis=0),
            jnp.concatenate(sides_of[index], axis=0),
        ]
        for index in range(3)
    ]

    keep = 1.0 - INNER_RATE * DECAY_RATE
    m_one = BETA_ONE * (1.0 - BETA_ONE) / (1.0 - BETA_ONE**2)
    m_two = (1.0 - BETA_ONE) / (1.0 - BETA_ONE**2)
    v_one = BETA_TWO * (1.0 - BETA_TWO) / (1.0 - BETA_TWO**2)
    v_two = (1.0 - BETA_TWO) / (1.0 - BETA_TWO**2)

    def first_update(w, g):
        return (
            keep * w.astype(F32) - INNER_RATE * (g / (jnp.abs(g) + epsilon))
        ).astype(BF16)

    def pseudo_gradient(weight, before, raw, scale):
        p = before.astype(F32)
        v = v_one * (p * p) + (v_two * scale * scale) * (raw * raw)
        first_low = jnp.abs(p) + epsilon
        second_low = v * lax.rsqrt(v + 1e-37) + epsilon
        moment = (INNER_RATE * m_one) * p + (INNER_RATE * m_two * scale) * raw
        top = (keep * INNER_RATE) * p * second_low + moment * first_low
        return (
            (1.0 - keep * keep) * weight.astype(F32) + top / (first_low * second_low)
        ).astype(BF16)

    def update_kernel(
        left, right, own_weight, near_weight, before, own_delta, near_delta, *, scale
    ):
        def write(weight, delta):
            for chunk in range(4):
                lines = pl.ds(chunk * (rows // 4), rows // 4)
                raw = contract_rows(left[:, lines], right[...])
                delta[lines] = pseudo_gradient(weight[lines], before[lines], raw, scale)

        @pl.when(pl.program_id(0) == 0)
        def _():
            write(near_weight, near_delta)

        @pl.when(pl.program_id(0) == 1)
        def _():
            write(own_weight, own_delta)

    def update(index, which, left, right, scale):
        deep = left.shape[0]
        whole = pl.BlockSpec((rows, width), lambda i: (0, 0))
        stacked = pl.BlockSpec((None, rows, width), lambda i: (index, 0, 0))
        return pl.pallas_call(
            functools.partial(update_kernel, scale=scale),
            grid=(2,),
            in_specs=[
                pl.BlockSpec((deep, rows), lambda i: (0, 1 - i)),
                pl.BlockSpec((deep, width), lambda i: (0, 0)),
                stacked,
                stacked,
                pl.BlockSpec((rows, width), lambda i: (1 - i, 0)),
            ],
            out_specs=[whole, whole],
            out_shape=[jax.ShapeDtypeStruct((rows, width), BF16)] * 2,
            cost_estimate=pl.CostEstimate(flops=1, bytes_accessed=1, transcendentals=0),
            compiler_params=pltpu.CompilerParams(vmem_limit_bytes=12 * 2**20),
        )(left, right, *((side, near_side) if which else (own, near)), first[index][which])

    def partial_pre(batch, w_gate, w_up):
        return jnp.stack(
            [
                jnp.dot(batch, w_gate, preferred_element_type=F32),
                jnp.dot(batch, w_up, preferred_element_type=F32),
            ]
        )

    def gated(pre):
        return (pre[0] * jax.nn.sigmoid(pre[0]) * pre[1]).astype(BF16)

    def output_sum(hidden, w_down):
        partial = contract_cols(hidden[0], w_down[0]) + contract_cols(
            hidden[1], w_down[1]
        )
        return sum_plane((partial * scale_hidden).astype(BF16))

    def hidden_partial(out_grad, w_down):
        return jnp.stack(
            [jnp.dot(out_grad, w, preferred_element_type=F32) for w in w_down]
        )

    def hidden_grads(partial, other, pre):
        hidden_grad = (partial + other.astype(F32)) * scale_hidden
        gate_pre, up_pre = pre[0], pre[1]
        sigma = jax.nn.sigmoid(gate_pre)
        gate_grad = (
            hidden_grad * up_pre * sigma * (1.0 + gate_pre * (1.0 - sigma))
        ).astype(BF16)
        up_grad = (hidden_grad * (gate_pre * sigma)).astype(BF16)
        return gate_grad, up_grad

    sides = range(2)
    partial = [partial_pre(batch_one, start[0][k], start[1][k]) for k in sides]
    def own_grad(step, total):
        return (
            flags[step] * (total - t_rows[step].astype(F32)) / total_rows
        ).astype(BF16)

    others = [other_half(item) for item in partial]
    batch_two = spread_plane(x_second)
    others = after(others, batch_two)
    pre = [(partial[k] + others[k].astype(F32)) * scale_in for k in sides]
    hidden = [gated(item) for item in pre]
    out_grad = spread_plane(own_grad(0, sum_height(output_sum(hidden, start[2]))))
    partial = hidden_partial(out_grad, start[2])
    other = other_half(partial)
    pairs = [hidden_grads(partial[k], other[k], pre[k]) for k in sides]
    grads = [
        [contract_rows(batch_one, pairs[k][0]) * scale_in for k in sides],
        [contract_rows(batch_one, pairs[k][1]) * scale_in for k in sides],
        [
            contract_rows(after(out_grad, partial), hidden[k]) * scale_hidden
            for k in sides
        ],
    ]
    weights = [[first_update(start[i][k], grads[i][k]) for k in sides] for i in range(3)]
    first = [[grads[i][k].astype(BF16) for k in sides] for i in range(3)]

    partial = [partial_pre(batch_two, weights[0][k], weights[1][k]) for k in sides]
    pre = [(item + other_half(item).astype(F32)) * scale_in for item in partial]
    hidden = [gated(item) for item in pre]
    out_grad = spread_plane(own_grad(1, sum_height(output_sum(hidden, weights[2]))))
    partial = [
        jnp.dot(out_grad, w, preferred_element_type=F32) for w in weights[2]
    ]
    other = [None, other_half(partial[1])]
    other[0] = other_half(after(partial[0], partial[1]))
    out_grad = after(out_grad, *partial)

    outer_own = (outer_gate, outer_up, outer_down)
    momenta = (momentum_gate, momentum_up, momentum_down)

    def both_cores(delta, near, *others):
        near = after(lax.ppermute(near, "c", SWAP), *others)
        return (delta.astype(F32) + near.astype(F32)).astype(BF16)

    delta = pseudo_gradient(
        start[2][1], first[2][1], contract_rows(out_grad, hidden[1]), scale_hidden
    )
    sent = both_cores(delta[:rows], delta[rows:])
    far_down = lax.ppermute(sent, "v", SWAP)
    pairs = [None, hidden_grads(partial[1], after(other[1], sent), pre[1])]
    sent_gate = both_cores(*update(0, 1, batch_two, pairs[1][0], scale_in))
    far_gate = lax.ppermute(sent_gate, "v", SWAP)
    sent_up = both_cores(*update(1, 1, batch_two, pairs[1][1], scale_in), far_down)
    far_up = lax.ppermute(sent_up, "v", SWAP)
    far = [far_gate, far_up, far_down]
    pairs[0] = hidden_grads(partial[0], after(other[0], sent_gate), pre[0])
    batch_two, out_grad = after((batch_two, out_grad), sent_gate, sent_up)
    new_params = [None] * 3
    new_momenta = [None] * 3
    for index, left, right, scale in (
        (2, out_grad, hidden[0], scale_hidden),
        (0, batch_two, pairs[0][0], scale_in),
        (1, batch_two, pairs[0][1], scale_in),
    ):
        own_delta, near_delta = update(index, 0, left, right, scale)
        near_delta = lax.ppermute(near_delta, "c", SWAP)
        total = (
            own_delta.astype(F32) + near_delta.astype(F32) + far[index].astype(F32)
        )
        average = total / 4.0
        fresh = MOMENTUM_RATE * momenta[index] + average
        new_momenta[index] = fresh
        new_params[index] = outer_own[index] - OUTER_RATE * (
            average + MOMENTUM_RATE * fresh
        )
    return tuple(new_params) + tuple(new_momenta)


def solution(mesh):
    fine = Mesh(mesh.devices.reshape(SIZES), AXES)
    rep, fsdp = AXES[:2], AXES[2:]
    state = P(rep, fsdp)
    rows = P(None, rep, fsdp, None)
    return jax.shard_map(
        per_device,
        mesh=fine,
        in_specs=(state,) * 6 + (rows, rows, P(None, rep, fsdp)),
        out_specs=(state,) * 6,
        check_vma=False,
    )
```
